32 devices in a mesh: groups: 2 (over y), st: 4 (over z), br: 2 (over x), pol: 2 (over core).
Axes of the slice: x: 2, y: 2, z: 4, core: 2. Of those that a mesh axis runs over, the one named last changes fastest.
Arguments:
- samples: bfloat16 [2, 1024, 32768], P(None, ('groups', 'st', 'pol'), 'br'), parts along dimension 1, may hold values from -6 to 6
- tap_table: int32 [12, 128], replicated, may hold values from -4096 to 4096
- station_flags: int32 [512], P(('st', 'pol')), may hold values 0 or 1
- beam_delays: int32 [512, 512], replicated, may hold values from 0 to 4095
Outputs:
- visibilities: float32 [1024, 128, 2, 512], P(('groups', 'br'), ('st', 'pol')), parts along dimension 0
- beam_series: float32 [1024, 256, 256], P(('groups', 'st', 'pol'), 'br'), parts along dimension 0
The draws below stay inside these ranges and needn't reach their ends.
There are 2 independent parts, one for each index of `groups`. The reference program is written for one: setup_inputs(seed, part) draws one part's arguments, and reference() takes and returns one part's arrays. A program takes and returns all parts, laid end to end along the dimension named above; an argument that names none is the same for every part. Nothing has to cross between parts.
All inputs are finite; a program needn't handle non-finite values. No bound on the sum of `station_flags` on one device may be relied on, other than what follows from the above.
Results may differ from the reference program's by a relative error of at most 0.012.
Values may be sent and summed in bfloat16 or wider, within the bound.
A program may use at most 128 MiB of HBM per device.

```python
import math
import jax
import jax.numpy as jnp
from jax import lax

NSP = 512
NCH = 128
NBEAM = 512
NTAP = 12
TS_DEV = 128
NT = 256
NSAMP = 32768
N_BR = 2


def place_ends(entries, key, least, high):
    dims = entries.shape
    index_at = [jax.random.randint(jax.random.fold_in(key, axis), (), 0, dims[axis]) for axis in range(len(dims))]
    entries = entries.at[tuple(index_at)].set(least)
    longest = dims.index(max(dims))
    index_at[longest] = (index_at[longest] + 1) % dims[longest]
    return entries.at[tuple(index_at)].set(high)


def steps_of(stream_key, extent, split, least, top_value):
    def one(axis_at, parts):
        steps = jax.random.uniform(jax.random.fold_in(jax.random.fold_in(stream_key, 6), axis_at), (parts,), jnp.float32, least / len(split), top_value / len(split))
        return jnp.repeat(jnp.exp(steps), extent[axis_at] // parts).reshape((-1,) + (1,) * (len(extent) - axis_at - 1))

    factor_of = one(*split[0])
    for cut in split[1:]:
        factor_of = factor_of * one(*cut)
    return factor_of


def scatter_about(rng, extent, deviation, bound, pieces=(), kind=jnp.bfloat16):
    level = steps_of(rng, extent, pieces, -0.22, 0.18) if pieces else 1.0
    drawn = jax.random.normal(rng, extent, jnp.float32) * deviation * level
    return jnp.minimum(jnp.maximum(drawn, -bound), bound).astype(kind)


def setup_inputs(seed: int = 0, part: int = 0) -> dict:
    seeds = jax.random.split(jax.random.key(seed), 5)
    own_keys = jax.random.split(jax.random.fold_in(seeds[4], part), 5)
    samples = scatter_about(own_keys[0], (2, NSP, NSAMP), 1.0, 6.0, ((1, 8), (2, 2)))
    tap_table = place_ends(jax.random.randint(seeds[1], (NTAP, NCH), -4096, 4097), jax.random.fold_in(seeds[1], 1), -4096, 4096).astype(jnp.int32)
    station_flags = place_ends((jax.random.randint(seeds[2], (NSP,), 0, 8) < 7).astype(jnp.int32), jax.random.fold_in(seeds[2], 1), 0, 1)
    beam_delays = place_ends(jax.random.randint(seeds[3], (NBEAM, NSP), 0, 4096), jax.random.fold_in(seeds[3], 1), 0, 4095).astype(jnp.int32)
    return {"samples": samples, "tap_table": tap_table, "station_flags": station_flags, "beam_delays": beam_delays}


tap_scale = 4096.0

def forward_table(nchan, per_owner):
    out_index = jnp.arange(2 * nchan)
    owner_block = out_index // (2 * per_owner)
    half_index = out_index // per_owner % 2
    channel = owner_block * per_owner + out_index % per_owner
    freq_index = jnp.arange(nchan)
    phase_index = freq_index[:, None] * channel[None, :] % nchan
    phase_angle = 2.0 * math.pi * phase_index.astype(jnp.float32) / nchan
    norm = 1.0 / math.sqrt(nchan)
    cos_part = jnp.cos(phase_angle) * norm
    sin_part = jnp.sin(phase_angle) * norm
    real_in = jnp.where(half_index[None, :] == 0, cos_part, -sin_part)
    imag_in = jnp.where(half_index[None, :] == 0, sin_part, cos_part)
    return jnp.stack([real_in, imag_in])

def inverse_table(nchan):
    out_index = jnp.arange(2 * nchan)
    sample = out_index % nchan
    half_index = out_index // nchan
    channel = jnp.arange(nchan)
    phase_index = channel[:, None] * sample[None, :] % nchan
    phase_angle = 2.0 * math.pi * phase_index.astype(jnp.float32) / nchan
    norm = 1.0 / math.sqrt(nchan)
    cos_part = jnp.cos(phase_angle) * norm
    sin_part = jnp.sin(phase_angle) * norm
    real_in = jnp.where(half_index[None, :] == 0, cos_part, sin_part)
    imag_in = jnp.where(half_index[None, :] == 0, -sin_part, cos_part)
    return jnp.stack([real_in, imag_in]).astype(jnp.bfloat16)

def beam_weights(beam_delays, channel_ids, ninputs, nchan):
    phase_index = beam_delays[None, :, :] * channel_ids[:, None, None] % nchan
    phase_angle = 2.0 * math.pi * phase_index.astype(jnp.float32) / nchan
    norm = 1.0 / math.sqrt(ninputs)
    weight_re = jnp.cos(phase_angle) * norm
    weight_im = -jnp.sin(phase_angle) * norm
    first_row = jnp.stack([weight_re, -weight_im], axis=1)
    second_row = jnp.stack([weight_im, weight_re], axis=1)
    return jnp.stack([first_row, second_row], axis=1).astype(jnp.bfloat16)

def reference(samples, tap_table, station_flags, beam_delays):
    coefficients = tap_table.astype(jnp.float32) / tap_scale
    table = forward_table(NCH, NCH)
    group = 8
    blocks = NSP // group
    sample_blocks = samples.reshape(2, blocks, group, NSAMP).transpose(1, 0, 2, 3)
    flag_blocks = station_flags.reshape(blocks, group)

    def filter_block(inputs):
        block, flag_block = inputs
        values = block.astype(jnp.float32).reshape(2, group, NT, NCH)
        extended = jnp.pad(values, ((0, 0), (0, 0), (NTAP - 1, 0), (0, 0)))
        filtered = jnp.zeros((2, group, NT, NCH), jnp.float32)
        for tap_index in range(NTAP):
            begin = NTAP - 1 - tap_index
            filtered = filtered + coefficients[tap_index][None, None, None, :] * extended[:, :, begin:begin + NT, :]
        spectra = jnp.einsum('rstk,rko->sot', filtered, table, precision=lax.Precision.HIGHEST)
        spectra = spectra * flag_block.astype(jnp.float32)[:, None, None]
        return spectra.astype(jnp.bfloat16)
    spectra = lax.map(filter_block, (sample_blocks, flag_blocks))
    spectra = spectra.reshape(NSP, 2, NCH, NT)
    time_scale = 1.0 / NT

    def channel_work(channel):
        chan_data = lax.dynamic_index_in_dim(spectra, channel, 2, keepdims=False).astype(jnp.float32)
        real_part = chan_data[:, 0].reshape(NSP, N_BR, TS_DEV).transpose(1, 0, 2)
        imag_part = chan_data[:, 1].reshape(NSP, N_BR, TS_DEV).transpose(1, 0, 2)
        right_side = jnp.concatenate([real_part, imag_part], axis=2)
        left_imag = jnp.concatenate([imag_part, -real_part], axis=2)
        vis_real = jnp.einsum('bik,bjk->bij', right_side, right_side) * time_scale
        vis_imag = jnp.einsum('bik,bjk->bij', left_imag, right_side) * time_scale
        vis_real = lax.optimization_barrier(jnp.sum(vis_real.astype(jnp.bfloat16).astype(jnp.float32), axis=0))
        vis_imag = lax.optimization_barrier(jnp.sum(vis_imag.astype(jnp.bfloat16).astype(jnp.float32), axis=0))
        vis_chan = jnp.stack([vis_real, vis_imag], axis=1)
        weights = beam_weights(beam_delays, channel[None].astype(jnp.int32), NSP, NCH)[0]
        beam_volt = jnp.einsum('orbi,irt->bot', weights.astype(jnp.float32), chan_data)
        return (vis_chan, beam_volt.astype(jnp.bfloat16))
    vis_all, beams = lax.map(channel_work, jnp.arange(NCH, dtype=jnp.int32))
    visibilities = vis_all.transpose(1, 0, 2, 3)
    synth_table = inverse_table(NCH).astype(jnp.float32)
    beam_group = 8

    def synth_block(block_index):
        start = (block_index * beam_group).astype(jnp.int32)
        piece = lax.dynamic_slice_in_dim(beams, start, beam_group, 1).astype(jnp.float32)
        return jnp.einsum('cbrt,rco->bto', piece, synth_table)
    series = lax.map(synth_block, jnp.arange(NBEAM // beam_group, dtype=jnp.int32))
    beam_series = series.reshape(NBEAM, NT, 2 * NCH)
    return (visibilities, beam_series)
```

```python
import functools
import math

import jax
import jax.numpy as jnp
from jax import lax
from jax.experimental import pallas as pl
from jax.experimental.pallas import tpu as pltpu
from jax.sharding import PartitionSpec as P

tap_scale = 4096.0
LANES = 128
GROUP = 16
VMEM = pltpu.VMEM


def forward_table(nchan, per_owner):
    out_index = jnp.arange(2 * nchan)
    owner_block = out_index // (2 * per_owner)
    half_index = out_index // per_owner % 2
    channel = owner_block * per_owner + out_index % per_owner
    freq_index = jnp.arange(nchan)
    phase_index = channel[:, None] * freq_index[None, :] % nchan
    phase_angle = 2.0 * math.pi * phase_index.astype(jnp.float32) / nchan
    norm = 1.0 / math.sqrt(nchan)
    cos_part = jnp.cos(phase_angle) * norm
    sin_part = jnp.sin(phase_angle) * norm
    real_in = jnp.where(half_index[:, None] == 0, cos_part, -sin_part)
    imag_in = jnp.where(half_index[:, None] == 0, sin_part, cos_part)
    return jnp.concatenate([real_in, imag_in], axis=1)


def inverse_table(nchan):
    out_index = jnp.arange(2 * nchan)
    sample = out_index % nchan
    half_index = out_index // nchan
    channel = jnp.arange(nchan)
    phase_index = channel[:, None] * sample[None, :] % nchan
    phase_angle = 2.0 * math.pi * phase_index.astype(jnp.float32) / nchan
    norm = 1.0 / math.sqrt(nchan)
    cos_part = jnp.cos(phase_angle) * norm
    sin_part = jnp.sin(phase_angle) * norm
    real_in = jnp.where(half_index[None, :] == 0, cos_part, sin_part)
    imag_in = jnp.where(half_index[None, :] == 0, -sin_part, cos_part)
    return jnp.stack([real_in, imag_in]).astype(jnp.bfloat16)


def filter_group(ntap, g, samples, before, coef, flags, table_hi, table_lo, ext, filt, turn):
    nspec = samples.shape[2] // LANES
    hist = ntap - 1
    rows = pl.ds(pl.multiple_of(g * GROUP, GROUP), GROUP)
    block = 8
    for r in range(2):
        for t in range(hist):
            ext[t] = before[r, rows, t * LANES : (t + 1) * LANES].astype(jnp.float32)

        @pl.loop(0, nspec // block)
        def _(tb):
            for u in range(block):
                t = tb * block + u
                lanes = pl.ds(pl.multiple_of(t * LANES, LANES), LANES)
                ext[hist + t] = samples[r, rows, lanes].astype(jnp.float32)

        for h in range(GROUP // 8):
            used = flags[pl.ds(pl.multiple_of(g * GROUP + h * 8, 8), 8), :]

            @pl.loop(0, nspec // block)
            def _(tb):
                t0 = tb * block
                window = [ext[t0 + u, h * 8 : h * 8 + 8, :] for u in range(block + hist)]
                for u in range(block):
                    total = coef[0:1, :] * window[hist + u]
                    for j in range(1, ntap):
                        total = total + coef[j : j + 1, :] * window[hist + u - j]
                    filt[r, pl.ds(h * 8 * nspec + t0 + u, 8, stride=nspec), :] = total * used

    @pl.loop(0, GROUP)
    def _(s):
        at = pl.ds(pl.multiple_of(s * nspec, nspec), nspec)
        values = jnp.concatenate([filt[0, at, :], filt[1, at, :]], axis=1)
        high = values.astype(jnp.bfloat16)
        low = (values - high.astype(jnp.float32)).astype(jnp.bfloat16)

        def product(a, b):
            return lax.dot_general(a, b, (((1,), (1,)), ((), ())), preferred_element_type=jnp.float32)

        out = product(table_lo[...], high) + product(table_hi[...], low) + product(table_hi[...], high)
        turn[pl.ds(s, out.shape[0], stride=GROUP), :] = out


def filter_kernel(ntap, samples, before, coef, flags, table_hi, table_lo, out, ext, filt, turn):
    nrow = out.shape[0]

    @pl.loop(0, samples.shape[1] // GROUP)
    def _(g):
        filter_group(ntap, g, samples, before, coef, flags, table_hi, table_lo, ext, filt, turn)
        rows = pl.ds(pl.multiple_of(g * GROUP, GROUP), GROUP)

        @pl.loop(0, nrow // 16)
        def _(o):
            part = turn[pl.ds(pl.multiple_of(o * 16 * GROUP, 16 * GROUP), 16 * GROUP), :]
            out[pl.ds(o * 16, 16), rows, :] = part.reshape(16, GROUP, LANES).astype(jnp.bfloat16)


def cosine(phase, nchan):
    z = (jnp.abs(phase - nchan // 2) - nchan // 4).astype(jnp.float32) * (2.0 * math.pi / nchan)
    z2 = z * z
    total = jnp.full_like(z, -1.0 / math.factorial(11))
    for n in (9, 7, 5, 3, 1):
        total = total * z2 + (-1.0) ** ((n - 1) // 2) / math.factorial(n)
    return total * z


def beam_kernel(nchan, delays, x, out, w_re, w_im, s_re, s_im):
    c = pl.program_id(0)
    per_owner = pl.num_programs(0)
    nbeam, nin = delays.shape
    mask = nchan - 1

    @pl.when(c == 0)
    def _():
        owner = lax.axis_index("st") * lax.axis_size("pol") + lax.axis_index("pol")
        d = delays[...]
        norm = 1.0 / math.sqrt(nin)
        step = d & mask
        s_re[...] = cosine(step, nchan)
        s_im[...] = -cosine((step - nchan // 4) & mask, nchan)
        first = (d * (owner * per_owner)) & mask
        w_re[...] = cosine(first, nchan) * norm
        w_im[...] = -cosine((first - nchan // 4) & mask, nchan) * norm

    re, im = w_re[...], w_im[...]
    left = jnp.concatenate([re.astype(jnp.bfloat16), (-im).astype(jnp.bfloat16)], axis=1)
    x_re, x_im = x[0, 0], x[1, 0]
    right = jnp.concatenate(
        [jnp.concatenate([x_re, x_im], axis=1), jnp.concatenate([x_im, -x_re], axis=1)], axis=0
    )
    volt = jnp.dot(left, right, preferred_element_type=jnp.float32).astype(jnp.bfloat16)
    nspec = x_re.shape[1]
    owners, per_beam = out.shape[0], out.shape[3]
    for o in range(owners):
        for r in range(2):
            out[o, 0, r] = volt[o * per_beam : (o + 1) * per_beam, r * nspec : (r + 1) * nspec]
    a, b = s_re[...], s_im[...]
    w_re[...] = re * a - im * b
    w_im[...] = re * b + im * a


def beams(beam_delays, turned, owners, nchan):
    _, per_owner, nin, nspec = turned.shape
    nbeam = beam_delays.shape[0]
    plane = pltpu.VMEM((nbeam, nin), jnp.float32)
    return pl.pallas_call(
        functools.partial(beam_kernel, nchan),
        grid=(per_owner,),
        out_shape=jax.ShapeDtypeStruct((owners, per_owner, 2, nbeam // owners, nspec), jnp.bfloat16),
        in_specs=[
            pl.BlockSpec((nbeam, nin), lambda c: (0, 0)),
            pl.BlockSpec((2, 1, nin, nspec), lambda c: (0, c, 0, 0)),
        ],
        out_specs=pl.BlockSpec((owners, 1, 2, nbeam // owners, nspec), lambda c: (0, c, 0, 0, 0)),
        scratch_shapes=[plane] * 4,
        compiler_params=pltpu.CompilerParams(vmem_limit_bytes=40 * 2**20),
        cost_estimate=pl.CostEstimate(flops=2**32, bytes_accessed=2**23, transcendentals=0),
    )(beam_delays, turned)


def local(samples, tap_table, station_flags, beam_delays):
    inputs_here = samples.shape[1]
    sample_count = samples.shape[2]
    ntap, nchan = tap_table.shape
    nin = beam_delays.shape[1]
    spectra_dev = sample_count // nchan
    owners = lax.axis_size("st") * lax.axis_size("pol")
    blocks = lax.axis_size("br")
    per_owner = nchan // owners
    tail_len = (ntap - 1) * nchan
    tail = samples[:, :, sample_count - tail_len :]
    before = lax.ppermute(tail, "br", [(i, i + 1) for i in range(blocks - 1)])
    coefficients = tap_table.astype(jnp.float32) / tap_scale
    flags = jnp.broadcast_to(station_flags.astype(jnp.float32)[:, None], (inputs_here, LANES))
    table = forward_table(nchan, per_owner)
    table_hi = table.astype(jnp.bfloat16)
    table_lo = (table - table_hi.astype(jnp.float32)).astype(jnp.bfloat16)
    spectra = pl.pallas_call(
        functools.partial(filter_kernel, ntap),
        out_shape=jax.ShapeDtypeStruct((2 * nchan, inputs_here, spectra_dev), jnp.bfloat16),
        scratch_shapes=[
            pltpu.VMEM((spectra_dev + ntap - 1, GROUP, LANES), jnp.float32),
            pltpu.VMEM((2, GROUP * spectra_dev, LANES), jnp.float32),
            pltpu.VMEM((2 * nchan * GROUP, LANES), jnp.float32),
        ],
        in_specs=[pl.BlockSpec(memory_space=VMEM)] * 6,
        out_specs=pl.BlockSpec(memory_space=VMEM),
        compiler_params=pltpu.CompilerParams(vmem_limit_bytes=40 * 2**20),
    )(samples, before, coefficients, flags, table_hi, table_lo)
    outgoing = spectra.reshape(owners, 2, per_owner, inputs_here, spectra_dev)
    arrived = lax.all_to_all(outgoing, ("st", "pol"), split_axis=0, concat_axis=3, tiled=True)
    turned = arrived.reshape(2, per_owner, nin, spectra_dev)

    volts = beams(beam_delays, turned, owners, nchan)
    series_in = lax.all_to_all(volts, ("st", "pol"), split_axis=0, concat_axis=0, tiled=True)

    parts = [turned]
    for k in range(1, blocks):
        parts.append(lax.ppermute(turned, "br", [(i, (i + k) % blocks) for i in range(blocks)]))
    right = jnp.concatenate([p[r] for p in parts for r in (0, 1)], axis=2)
    left_imag = jnp.concatenate([q for p in parts for q in (p[1], -p[0])], axis=2)
    rows_here = nin // blocks
    first_row = lax.axis_index("br") * rows_here
    left = lax.dynamic_slice_in_dim(right, first_row, rows_here, 1)
    left_imag = lax.dynamic_slice_in_dim(left_imag, first_row, rows_here, 1)
    time_scale = 1.0 / (spectra_dev * blocks)
    vis_real = jnp.einsum("cik,cjk->icj", left, right, preferred_element_type=jnp.float32)
    vis_imag = jnp.einsum("cik,cjk->icj", left_imag, right, preferred_element_type=jnp.float32)
    visibilities = jnp.stack([vis_real, vis_imag], axis=2) * time_scale

    series_in = series_in.reshape(nchan, 2, -1, spectra_dev)
    beam_series = jnp.einsum(
        "crbt,rcn->btn", series_in, inverse_table(nchan), preferred_element_type=jnp.float32
    )
    return (visibilities, beam_series)


def solution(mesh):
    return jax.shard_map(
        local,
        mesh=mesh,
        in_specs=(P(None, ("groups", "st", "pol"), "br"), P(), P(("st", "pol")), P()),
        out_specs=(
            P(("groups", "br"), ("st", "pol"), None, None),
            P(("groups", "st", "pol"), "br", None),
        ),
        check_vma=False,
    )
```

```python
import functools
import math

import jax
import jax.numpy as jnp
from jax import lax
from jax.experimental import pallas as pl
from jax.experimental.pallas import tpu as pltpu
from jax.sharding import PartitionSpec as P

tap_scale = 4096.0
LANES = 128
GROUP = 16
VMEM = pltpu.VMEM
MESH = pl.DeviceIdType.MESH


def forward_table(nchan, per_owner):
    out_index = jnp.arange(2 * nchan)
    owner_block = out_index // (2 * per_owner)
    half_index = out_index // per_owner % 2
    channel = owner_block * per_owner + out_index % per_owner
    freq_index = jnp.arange(nchan)
    phase_index = channel[:, None] * freq_index[None, :] % nchan
    phase_angle = 2.0 * math.pi * phase_index.astype(jnp.float32) / nchan
    norm = 1.0 / math.sqrt(nchan)
    cos_part = jnp.cos(phase_angle) * norm
    sin_part = jnp.sin(phase_angle) * norm
    real_in = jnp.where(half_index[:, None] == 0, cos_part, -sin_part)
    imag_in = jnp.where(half_index[:, None] == 0, sin_part, cos_part)
    return jnp.concatenate([real_in, imag_in], axis=1)


def inverse_table(nchan):
    out_index = jnp.arange(2 * nchan)
    sample = out_index % nchan
    half_index = out_index // nchan
    channel = jnp.arange(nchan)
    phase_index = channel[:, None] * sample[None, :] % nchan
    phase_angle = 2.0 * math.pi * phase_index.astype(jnp.float32) / nchan
    norm = 1.0 / math.sqrt(nchan)
    cos_part = jnp.cos(phase_angle) * norm
    sin_part = jnp.sin(phase_angle) * norm
    real_in = jnp.where(half_index[None, :] == 0, cos_part, sin_part)
    imag_in = jnp.where(half_index[None, :] == 0, -sin_part, cos_part)
    return jnp.stack([real_in, imag_in]).astype(jnp.bfloat16)


def filter_group(ntap, g, samples, before, coef, flags, table_hi, table_lo, ext, filt, turn):
    nspec = samples.shape[2] // LANES
    hist = ntap - 1
    rows = pl.ds(pl.multiple_of(g * GROUP, GROUP), GROUP)
    block = 8
    for r in range(2):
        for t in range(hist):
            past = before[r, rows, t * LANES : (t + 1) * LANES].astype(jnp.float32)
            ext[t] = jnp.where(lax.axis_index("br") > 0, past, 0.0)

        @pl.loop(0, nspec // block)
        def _(tb):
            for u in range(block):
                t = tb * block + u
                lanes = pl.ds(pl.multiple_of(t * LANES, LANES), LANES)
                ext[hist + t] = samples[r, rows, lanes].astype(jnp.float32)

        for h in range(GROUP // 8):
            used = flags[pl.ds(pl.multiple_of(g * GROUP + h * 8, 8), 8), :]

            @pl.loop(0, nspec // block)
            def _(tb):
                t0 = tb * block
                window = [ext[t0 + u, h * 8 : h * 8 + 8, :] for u in range(block + hist)]
                for u in range(block):
                    total = coef[0:1, :] * window[hist + u]
                    for j in range(1, ntap):
                        total = total + coef[j : j + 1, :] * window[hist + u - j]
                    filt[r, pl.ds(h * 8 * nspec + t0 + u, 8, stride=nspec), :] = total * used

    @pl.loop(0, GROUP)
    def _(s):
        at = pl.ds(pl.multiple_of(s * nspec, nspec), nspec)
        values = jnp.concatenate([filt[0, at, :], filt[1, at, :]], axis=1)
        high = values.astype(jnp.bfloat16)
        low = (values - high.astype(jnp.float32)).astype(jnp.bfloat16)

        def product(a, b):
            return lax.dot_general(a, b, (((1,), (1,)), ((), ())), preferred_element_type=jnp.float32)

        out = product(table_lo[...], high) + product(table_hi[...], low) + product(table_hi[...], high)
        turn[pl.ds(s, out.shape[0], stride=GROUP), :] = out


def turn_kernel(
    ntap, samples, coef, flags, table_hi, table_lo, turned, others,
    before, send, ext, filt, turn,
    halo_send, halo_recv, turn_send, turn_recv, share_send, share_recv,
):
    nrow, inputs_here = send.shape[0], send.shape[1]
    groups = inputs_here // GROUP
    npol = lax.axis_size("pol")
    owners = lax.axis_size("st") * npol
    blocks = lax.axis_size("br")
    me = lax.axis_index("st") * npol + lax.axis_index("pol")
    slot = lax.axis_index("br")
    own_rows = nrow // owners
    tail = before.shape[2]
    begin = samples.shape[2] - tail

    def owner_id(o):
        return {"st": o // npol, "pol": lax.rem(o, npol)}

    def block_id(step):
        return {"br": lax.rem(slot + step, blocks)}

    barrier = pltpu.get_barrier_semaphore()
    for k in range(1, owners):
        pl.semaphore_signal(barrier, inc=1, device_id=owner_id(lax.rem(me + k, owners)), device_id_type=MESH)
    for k in range(1, blocks):
        pl.semaphore_signal(barrier, inc=1, device_id=block_id(k), device_id_type=MESH)
    pl.semaphore_wait(barrier, owners + blocks - 2)

    def rows_of(g):
        return pl.ds(pl.multiple_of(g * GROUP, GROUP), GROUP)

    def place(owner, g):
        return pl.ds(pl.multiple_of(owner * inputs_here + g * GROUP, GROUP), GROUP)

    def halo(g):
        return pltpu.make_async_remote_copy(
            src_ref=samples.at[:, rows_of(g), pl.ds(begin, tail)],
            dst_ref=before.at[:, rows_of(g), :],
            send_sem=halo_send.at[g],
            recv_sem=halo_recv.at[g],
            device_id=block_id(1),
            device_id_type=MESH,
        )

    def corner(g, k):
        target = lax.rem(me + k, owners)
        return pltpu.make_async_remote_copy(
            src_ref=send.at[pl.ds(target * own_rows, own_rows), rows_of(g), :],
            dst_ref=turned.at[:, place(me, g), :],
            send_sem=turn_send.at[g, k],
            recv_sem=turn_recv.at[g, k],
            device_id=owner_id(target),
            device_id_type=MESH,
        )

    def share(g, k, step):
        at = place(lax.rem(me + owners - k, owners), g)
        return pltpu.make_async_remote_copy(
            src_ref=turned.at[:, at, :],
            dst_ref=others.at[step - 1, :, at, :],
            send_sem=share_send.at[g, k, step - 1],
            recv_sem=share_recv.at[g, k, step - 1],
            device_id=block_id(step),
            device_id_type=MESH,
        )

    @pl.loop(0, groups)
    def _(g):
        halo(g).start()

    def drain(g):
        @pl.loop(1, owners)
        def _(k):
            corner(g, k).wait_recv()
            for step in range(1, blocks):
                share(g, k, step).start()

    @pl.loop(0, groups)
    def _(g):
        halo(g).wait_recv()
        filter_group(ntap, g, samples, before, coef, flags, table_hi, table_lo, ext, filt, turn)

        @pl.loop(0, nrow // own_rows)
        def _(o):
            size = own_rows * GROUP
            part = turn[pl.ds(pl.multiple_of(o * size, size), size), :]
            send[pl.ds(o * own_rows, own_rows), rows_of(g), :] = part.reshape(
                own_rows, GROUP, LANES
            ).astype(jnp.bfloat16)

        @pl.loop(1, owners)
        def _(k):
            corner(g, k).start()

        turned[:, place(me, g), :] = send[pl.ds(me * own_rows, own_rows), rows_of(g), :]
        for step in range(1, blocks):
            share(g, 0, step).start()

        @pl.when(g >= 2)
        def _():
            drain(g - 2)

    for g in range(max(groups - 2, 0), groups):
        drain(g)

    @pl.loop(0, groups)
    def _(g):
        halo(g).wait_send()

        @pl.loop(1, owners)
        def _(k):
            corner(g, k).wait_send()

        @pl.loop(0, owners)
        def _(k):
            for step in range(1, blocks):
                share(g, k, step).wait()


def cosine(phase, nchan):
    z = (jnp.abs(phase - nchan // 2) - nchan // 4).astype(jnp.float32) * (2.0 * math.pi / nchan)
    z2 = z * z
    total = jnp.full_like(z, -1.0 / math.factorial(11))
    for n in (9, 7, 5, 3, 1):
        total = total * z2 + (-1.0) ** ((n - 1) // 2) / math.factorial(n)
    return total * z


def beam_kernel(nchan, delays, x, out, w_re, w_im, s_re, s_im):
    c = pl.program_id(0)
    per_owner = pl.num_programs(0)
    nbeam, nin = delays.shape
    mask = nchan - 1

    @pl.when(c == 0)
    def _():
        owner = lax.axis_index("st") * lax.axis_size("pol") + lax.axis_index("pol")
        d = delays[...]
        norm = 1.0 / math.sqrt(nin)
        step = d & mask
        s_re[...] = cosine(step, nchan)
        s_im[...] = -cosine((step - nchan // 4) & mask, nchan)
        first = (d * (owner * per_owner)) & mask
        w_re[...] = cosine(first, nchan) * norm
        w_im[...] = -cosine((first - nchan // 4) & mask, nchan) * norm

    re, im = w_re[...], w_im[...]
    left = jnp.concatenate([re.astype(jnp.bfloat16), (-im).astype(jnp.bfloat16)], axis=1)
    x_re, x_im = x[0, 0], x[1, 0]
    right = jnp.concatenate(
        [jnp.concatenate([x_re, x_im], axis=1), jnp.concatenate([x_im, -x_re], axis=1)], axis=0
    )
    volt = jnp.dot(left, right, preferred_element_type=jnp.float32).astype(jnp.bfloat16)
    nspec = x_re.shape[1]
    owners, per_beam = out.shape[0], out.shape[3]
    for o in range(owners):
        for r in range(2):
            out[o, 0, r] = volt[o * per_beam : (o + 1) * per_beam, r * nspec : (r + 1) * nspec]
    a, b = s_re[...], s_im[...]
    w_re[...] = re * a - im * b
    w_im[...] = re * b + im * a


def beams(beam_delays, turned, owners, nchan):
    _, per_owner, nin, nspec = turned.shape
    nbeam = beam_delays.shape[0]
    plane = pltpu.VMEM((nbeam, nin), jnp.float32)
    return pl.pallas_call(
        functools.partial(beam_kernel, nchan),
        grid=(per_owner,),
        out_shape=jax.ShapeDtypeStruct((owners, per_owner, 2, nbeam // owners, nspec), jnp.bfloat16),
        in_specs=[
            pl.BlockSpec((nbeam, nin), lambda c: (0, 0)),
            pl.BlockSpec((2, 1, nin, nspec), lambda c: (0, c, 0, 0)),
        ],
        out_specs=pl.BlockSpec((owners, 1, 2, nbeam // owners, nspec), lambda c: (0, c, 0, 0, 0)),
        scratch_shapes=[plane] * 4,
        compiler_params=pltpu.CompilerParams(vmem_limit_bytes=40 * 2**20),
        cost_estimate=pl.CostEstimate(flops=2**32, bytes_accessed=2**23, transcendentals=0),
    )(beam_delays, turned)


def local(samples, tap_table, station_flags, beam_delays):
    inputs_here = samples.shape[1]
    sample_count = samples.shape[2]
    ntap, nchan = tap_table.shape
    nin = beam_delays.shape[1]
    spectra_dev = sample_count // nchan
    owners = lax.axis_size("st") * lax.axis_size("pol")
    blocks = lax.axis_size("br")
    per_owner = nchan // owners
    coefficients = tap_table.astype(jnp.float32) / tap_scale
    flags = jnp.broadcast_to(station_flags.astype(jnp.float32)[:, None], (inputs_here, LANES))
    table = forward_table(nchan, per_owner)
    table_hi = table.astype(jnp.bfloat16)
    table_lo = (table - table_hi.astype(jnp.float32)).astype(jnp.bfloat16)
    groups = inputs_here // GROUP
    dma = pltpu.SemaphoreType.DMA
    turned, others = pl.pallas_call(
        functools.partial(turn_kernel, ntap),
        out_shape=(
            jax.ShapeDtypeStruct((2 * per_owner, nin, spectra_dev), jnp.bfloat16),
            jax.ShapeDtypeStruct((blocks - 1, 2 * per_owner, nin, spectra_dev), jnp.bfloat16),
        ),
        scratch_shapes=[
            pltpu.VMEM((2, inputs_here, (ntap - 1) * nchan), jnp.bfloat16),
            pltpu.VMEM((2 * nchan, inputs_here, spectra_dev), jnp.bfloat16),
            pltpu.VMEM((spectra_dev + ntap - 1, GROUP, LANES), jnp.float32),
            pltpu.VMEM((2, GROUP * spectra_dev, LANES), jnp.float32),
            pltpu.VMEM((2 * nchan * GROUP, LANES), jnp.float32),
            dma((groups,)),
            dma((groups,)),
            dma((groups, owners)),
            dma((groups, owners)),
            dma((groups, owners, blocks - 1)),
            dma((groups, owners, blocks - 1)),
        ],
        in_specs=[pl.BlockSpec(memory_space=VMEM)] * 5,
        out_specs=(pl.BlockSpec(memory_space=VMEM), pl.BlockSpec(memory_space=VMEM)),
        compiler_params=pltpu.CompilerParams(
            vmem_limit_bytes=40 * 2**20, collective_id=0, has_side_effects=True
        ),
    )(samples, coefficients, flags, table_hi, table_lo)
    turned = turned.reshape(2, per_owner, nin, spectra_dev)
    others = others.reshape(blocks - 1, 2, per_owner, nin, spectra_dev)

    volts = beams(beam_delays, turned, owners, nchan)
    series_in = lax.all_to_all(volts, ("st", "pol"), split_axis=0, concat_axis=0, tiled=True)

    parts = [turned] + [others[k] for k in range(blocks - 1)]
    right = jnp.concatenate([p[r] for p in parts for r in (0, 1)], axis=2)
    left_imag = jnp.concatenate([q for p in parts for q in (p[1], -p[0])], axis=2)
    rows_here = nin // blocks
    first_row = lax.axis_index("br") * rows_here
    left = lax.dynamic_slice_in_dim(right, first_row, rows_here, 1)
    left_imag = lax.dynamic_slice_in_dim(left_imag, first_row, rows_here, 1)
    time_scale = 1.0 / (spectra_dev * blocks)
    vis_real = jnp.einsum("cik,cjk->icj", left, right, preferred_element_type=jnp.float32)
    vis_imag = jnp.einsum("cik,cjk->icj", left_imag, right, preferred_element_type=jnp.float32)
    visibilities = jnp.stack([vis_real, vis_imag], axis=2) * time_scale

    series_in = series_in.reshape(nchan, 2, -1, spectra_dev)
    beam_series = jnp.einsum(
        "crbt,rcn->btn", series_in, inverse_table(nchan), preferred_element_type=jnp.float32
    )
    return (visibilities, beam_series)


def solution(mesh):
    return jax.shard_map(
        local,
        mesh=mesh,
        in_specs=(P(None, ("groups", "st", "pol"), "br"), P(), P(("st", "pol")), P()),
        out_specs=(
            P(("groups", "br"), ("st", "pol"), None, None),
            P(("groups", "st", "pol"), "br", None),
        ),
        check_vma=False,
    )
```

```python
import functools
import math

import jax
import jax.numpy as jnp
from jax import lax
from jax.experimental import pallas as pl
from jax.experimental.pallas import tpu as pltpu
from jax.sharding import PartitionSpec as P

tap_scale = 4096.0
LANES = 128
GROUP = 16
VMEM = pltpu.VMEM
MESH = pl.DeviceIdType.MESH


def forward_table(nchan, per_owner):
    out_index = jnp.arange(2 * nchan)
    owner_block = out_index // (2 * per_owner)
    half_index = out_index // per_owner % 2
    channel = owner_block * per_owner + out_index % per_owner
    freq_index = jnp.arange(nchan)
    phase_index = channel[:, None] * freq_index[None, :] % nchan
    phase_angle = 2.0 * math.pi * phase_index.astype(jnp.float32) / nchan
    norm = 1.0 / math.sqrt(nchan)
    cos_part = jnp.cos(phase_angle) * norm
    sin_part = jnp.sin(phase_angle) * norm
    real_in = jnp.where(half_index[:, None] == 0, cos_part, -sin_part)
    imag_in = jnp.where(half_index[:, None] == 0, sin_part, cos_part)
    return jnp.concatenate([real_in, imag_in], axis=1)


def inverse_table(nchan):
    out_index = jnp.arange(2 * nchan)
    sample = out_index % nchan
    half_index = out_index // nchan
    channel = jnp.arange(nchan)
    phase_index = channel[:, None] * sample[None, :] % nchan
    phase_angle = 2.0 * math.pi * phase_index.astype(jnp.float32) / nchan
    norm = 1.0 / math.sqrt(nchan)
    cos_part = jnp.cos(phase_angle) * norm
    sin_part = jnp.sin(phase_angle) * norm
    real_in = jnp.where(half_index[None, :] == 0, cos_part, sin_part)
    imag_in = jnp.where(half_index[None, :] == 0, -sin_part, cos_part)
    return jnp.stack([real_in, imag_in]).astype(jnp.bfloat16)


def filter_group(ntap, g, samples, before, coef, flags, table_hi, table_lo, ext, filt, turn):
    nspec = samples.shape[2] // LANES
    hist = ntap - 1
    rows = pl.ds(pl.multiple_of(g * GROUP, GROUP), GROUP)
    block = 8
    for r in range(2):
        for t in range(hist):
            past = before[r, rows, t * LANES : (t + 1) * LANES].astype(jnp.float32)
            ext[t] = jnp.where(lax.axis_index("br") > 0, past, 0.0)

        @pl.loop(0, nspec // block)
        def _(tb):
            for u in range(block):
                t = tb * block + u
                lanes = pl.ds(pl.multiple_of(t * LANES, LANES), LANES)
                ext[hist + t] = samples[r, rows, lanes].astype(jnp.float32)

        for h in range(GROUP // 8):
            used = flags[pl.ds(pl.multiple_of(g * GROUP + h * 8, 8), 8), :]

            @pl.loop(0, nspec // block)
            def _(tb):
                t0 = tb * block
                window = [ext[t0 + u, h * 8 : h * 8 + 8, :] for u in range(block + hist)]
                for u in range(block):
                    total = coef[0:1, :] * window[hist + u]
                    for j in range(1, ntap):
                        total = total + coef[j : j + 1, :] * window[hist + u - j]
                    filt[r, pl.ds(h * 8 * nspec + t0 + u, 8, stride=nspec), :] = total * used

    @pl.loop(0, GROUP)
    def _(s):
        at = pl.ds(pl.multiple_of(s * nspec, nspec), nspec)
        values = jnp.concatenate([filt[0, at, :], filt[1, at, :]], axis=1)
        high = values.astype(jnp.bfloat16)
        low = (values - high.astype(jnp.float32)).astype(jnp.bfloat16)

        def product(a, b):
            return lax.dot_general(a, b, (((1,), (1,)), ((), ())), preferred_element_type=jnp.float32)

        out = product(table_lo[...], high) + product(table_hi[...], low) + product(table_hi[...], high)
        turn[pl.ds(s, out.shape[0], stride=GROUP), :] = out


def turn_kernel(
    ntap, samples, coef, flags, table_hi, table_lo, delays, turned, others, volts,
    before, send, ext, filt, turn, weights, w_re, w_im, s_re, s_im,
    halo_send, halo_recv, turn_send, turn_recv, share_send, share_recv,
):
    nrow, inputs_here = send.shape[0], send.shape[1]
    groups = inputs_here // GROUP
    npol = lax.axis_size("pol")
    owners = lax.axis_size("st") * npol
    blocks = lax.axis_size("br")
    me = lax.axis_index("st") * npol + lax.axis_index("pol")
    slot = lax.axis_index("br")
    own_rows = nrow // owners
    tail = before.shape[2]
    begin = samples.shape[2] - tail

    def owner_id(o):
        return {"st": o // npol, "pol": lax.rem(o, npol)}

    def block_id(step):
        return {"br": lax.rem(slot + step, blocks)}

    barrier = pltpu.get_barrier_semaphore()
    for k in range(1, owners):
        pl.semaphore_signal(barrier, inc=1, device_id=owner_id(lax.rem(me + k, owners)), device_id_type=MESH)
    for k in range(1, blocks):
        pl.semaphore_signal(barrier, inc=1, device_id=block_id(k), device_id_type=MESH)
    pl.semaphore_wait(barrier, owners + blocks - 2)

    def rows_of(g):
        return pl.ds(pl.multiple_of(g * GROUP, GROUP), GROUP)

    def place(owner, g):
        return pl.ds(pl.multiple_of(owner * inputs_here + g * GROUP, GROUP), GROUP)

    def halo(g):
        return pltpu.make_async_remote_copy(
            src_ref=samples.at[:, rows_of(g), pl.ds(begin, tail)],
            dst_ref=before.at[:, rows_of(g), :],
            send_sem=halo_send.at[g],
            recv_sem=halo_recv.at[g],
            device_id=block_id(1),
            device_id_type=MESH,
        )

    def corner(g, k):
        target = lax.rem(me + k, owners)
        return pltpu.make_async_remote_copy(
            src_ref=send.at[pl.ds(target * own_rows, own_rows), rows_of(g), :],
            dst_ref=turned.at[:, place(me, g), :],
            send_sem=turn_send.at[g, k],
            recv_sem=turn_recv.at[g, k],
            device_id=owner_id(target),
            device_id_type=MESH,
        )

    def share(g, k, step):
        at = place(lax.rem(me + owners - k, owners), g)
        return pltpu.make_async_remote_copy(
            src_ref=turned.at[:, at, :],
            dst_ref=others.at[step - 1, :, at, :],
            send_sem=share_send.at[g, k, step - 1],
            recv_sem=share_recv.at[g, k, step - 1],
            device_id=block_id(step),
            device_id_type=MESH,
        )

    @pl.loop(0, groups)
    def _(g):
        halo(g).start()

    def drain(g):
        @pl.loop(1, owners)
        def _(k):
            corner(g, k).wait_recv()
            for step in range(1, blocks):
                share(g, k, step).start()

    @pl.loop(0, groups)
    def _(g):
        halo(g).wait_recv()
        filter_group(ntap, g, samples, before, coef, flags, table_hi, table_lo, ext, filt, turn)

        @pl.loop(0, nrow // own_rows)
        def _(o):
            size = own_rows * GROUP
            part = turn[pl.ds(pl.multiple_of(o * size, size), size), :]
            send[pl.ds(o * own_rows, own_rows), rows_of(g), :] = part.reshape(
                own_rows, GROUP, LANES
            ).astype(jnp.bfloat16)

        @pl.loop(1, owners)
        def _(k):
            corner(g, k).start()

        turned[:, place(me, g), :] = send[pl.ds(me * own_rows, own_rows), rows_of(g), :]
        for step in range(1, blocks):
            share(g, 0, step).start()

        @pl.when(g >= 2)
        def _():
            drain(g - 2)

    make_weights(me, nrow // 2, own_rows // 2, delays, weights, w_re, w_im, s_re, s_im)

    for g in range(max(groups - 2, 0), groups):
        drain(g)

    form_beams(turned, weights, volts)

    @pl.loop(0, groups)
    def _(g):
        halo(g).wait_send()

        @pl.loop(1, owners)
        def _(k):
            corner(g, k).wait_send()

        @pl.loop(0, owners)
        def _(k):
            for step in range(1, blocks):
                share(g, k, step).wait()


def cosine(phase, nchan):
    z = (jnp.abs(phase - nchan // 2) - nchan // 4).astype(jnp.float32) * (2.0 * math.pi / nchan)
    z2 = z * z
    total = jnp.full_like(z, -1.0 / math.factorial(11))
    for n in (9, 7, 5, 3, 1):
        total = total * z2 + (-1.0) ** ((n - 1) // 2) / math.factorial(n)
    return total * z


def make_weights(owner, nchan, per_owner, delays, weights, w_re, w_im, s_re, s_im):
    nin = delays.shape[1]
    mask = nchan - 1
    norm = 1.0 / math.sqrt(nin)
    d = delays[...]
    step = d & mask
    s_re[...] = cosine(step, nchan)
    s_im[...] = -cosine((step - nchan // 4) & mask, nchan)
    first = (d * (owner * per_owner)) & mask
    w_re[...] = cosine(first, nchan) * norm
    w_im[...] = -cosine((first - nchan // 4) & mask, nchan) * norm

    @pl.loop(0, per_owner)
    def _(c):
        re, im = w_re[...], w_im[...]
        weights[c, :, :nin] = re.astype(jnp.bfloat16)
        weights[c, :, nin:] = (-im).astype(jnp.bfloat16)
        a, b = s_re[...], s_im[...]
        w_re[...] = re * a - im * b
        w_im[...] = re * b + im * a


def form_beams(turned, weights, volts):
    owners, per_owner, _, per_beam, nspec = volts.shape

    @pl.loop(0, per_owner)
    def _(c):
        x_re, x_im = turned[c], turned[per_owner + c]
        right = jnp.concatenate(
            [jnp.concatenate([x_re, x_im], axis=1), jnp.concatenate([x_im, -x_re], axis=1)], axis=0
        )
        volt = jnp.dot(weights[c], right, preferred_element_type=jnp.float32).astype(jnp.bfloat16)
        for o in range(owners):
            for r in range(2):
                volts[o, c, r] = volt[o * per_beam : (o + 1) * per_beam, r * nspec : (r + 1) * nspec]


def local(samples, tap_table, station_flags, beam_delays):
    inputs_here = samples.shape[1]
    sample_count = samples.shape[2]
    ntap, nchan = tap_table.shape
    nin = beam_delays.shape[1]
    spectra_dev = sample_count // nchan
    owners = lax.axis_size("st") * lax.axis_size("pol")
    blocks = lax.axis_size("br")
    per_owner = nchan // owners
    coefficients = tap_table.astype(jnp.float32) / tap_scale
    flags = jnp.broadcast_to(station_flags.astype(jnp.float32)[:, None], (inputs_here, LANES))
    table = forward_table(nchan, per_owner)
    table_hi = table.astype(jnp.bfloat16)
    table_lo = (table - table_hi.astype(jnp.float32)).astype(jnp.bfloat16)
    groups = inputs_here // GROUP
    dma = pltpu.SemaphoreType.DMA
    nbeam = beam_delays.shape[0]
    plane = pltpu.VMEM((nbeam, nin), jnp.float32)
    turned, others, volts = pl.pallas_call(
        functools.partial(turn_kernel, ntap),
        out_shape=(
            jax.ShapeDtypeStruct((2 * per_owner, nin, spectra_dev), jnp.bfloat16),
            jax.ShapeDtypeStruct((blocks - 1, 2 * per_owner, nin, spectra_dev), jnp.bfloat16),
            jax.ShapeDtypeStruct((owners, per_owner, 2, nbeam // owners, spectra_dev), jnp.bfloat16),
        ),
        scratch_shapes=[
            pltpu.VMEM((2, inputs_here, (ntap - 1) * nchan), jnp.bfloat16),
            pltpu.VMEM((2 * nchan, inputs_here, spectra_dev), jnp.bfloat16),
            pltpu.VMEM((spectra_dev + ntap - 1, GROUP, LANES), jnp.float32),
            pltpu.VMEM((2, GROUP * spectra_dev, LANES), jnp.float32),
            pltpu.VMEM((2 * nchan * GROUP, LANES), jnp.float32),
            pltpu.VMEM((per_owner, nbeam, 2 * nin), jnp.bfloat16),
            plane,
            plane,
            plane,
            plane,
            dma((groups,)),
            dma((groups,)),
            dma((groups, owners)),
            dma((groups, owners)),
            dma((groups, owners, blocks - 1)),
            dma((groups, owners, blocks - 1)),
        ],
        in_specs=[pl.BlockSpec(memory_space=VMEM)] * 6,
        out_specs=(pl.BlockSpec(memory_space=VMEM),) * 3,
        compiler_params=pltpu.CompilerParams(
            vmem_limit_bytes=54 * 2**20, collective_id=0, has_side_effects=True
        ),
    )(samples, coefficients, flags, table_hi, table_lo, beam_delays)
    turned = turned.reshape(2, per_owner, nin, spectra_dev)
    others = others.reshape(blocks - 1, 2, per_owner, nin, spectra_dev)

    series_in = lax.all_to_all(volts, ("st", "pol"), split_axis=0, concat_axis=0, tiled=True)

    parts = [turned] + [others[k] for k in range(blocks - 1)]
    right = jnp.concatenate([p[r] for p in parts for r in (0, 1)], axis=2)
    left_imag = jnp.concatenate([q for p in parts for q in (p[1], -p[0])], axis=2)
    rows_here = nin // blocks
    first_row = lax.axis_index("br") * rows_here
    left = lax.dynamic_slice_in_dim(right, first_row, rows_here, 1)
    left_imag = lax.dynamic_slice_in_dim(left_imag, first_row, rows_here, 1)
    time_scale = 1.0 / (spectra_dev * blocks)
    vis_real = jnp.einsum("cik,cjk->icj", left, right, preferred_element_type=jnp.float32)
    vis_imag = jnp.einsum("cik,cjk->icj", left_imag, right, preferred_element_type=jnp.float32)
    visibilities = jnp.stack([vis_real, vis_imag], axis=2) * time_scale

    series_in = series_in.reshape(nchan, 2, -1, spectra_dev)
    beam_series = jnp.einsum(
        "crbt,rcn->btn", series_in, inverse_table(nchan), preferred_element_type=jnp.float32
    )
    return (visibilities, beam_series)


def solution(mesh):
    return jax.shard_map(
        local,
        mesh=mesh,
        in_specs=(P(None, ("groups", "st", "pol"), "br"), P(), P(("st", "pol")), P()),
        out_specs=(
            P(("groups", "br"), ("st", "pol"), None, None),
            P(("groups", "st", "pol"), "br", None),
        ),
        check_vma=False,
    )
```
